512 devices in a mesh: clips: 4 (over x), tm: 8 (over y), tile: 16 (over z, core).
Axes of the slice: x: 4, y: 8, z: 8, core: 2. Of those that a mesh axis runs over, the one named last changes fastest.
Arguments:
- video: bfloat16 [4, 32, 96, 64, 256], P('clips', 'tm', None, 'tile')
- norm1_gain: float32 [96], replicated, may hold values from 0.1 to 1.9
- conv1_weight: bfloat16 [3, 3, 3, 96, 96], replicated, may hold values from -0.21875 to 0.21875
- conv1_bias: float32 [96], replicated, may hold values from -3 to 3
- norm2_gain: float32 [96], replicated, may hold values from 0.1 to 1.9
- conv2_weight: bfloat16 [3, 3, 3, 96, 96], replicated, may hold values from -0.21875 to 0.21875
- conv2_bias: float32 [96], replicated, may hold values from -3 to 3
- down_weight: bfloat16 [3, 3, 96, 96], replicated, may hold values from -0.21875 to 0.21875
- down_bias: float32 [96], replicated, may hold values from -3 to 3
- proj_weight: bfloat16 [192, 96], replicated, may hold values from -0.625 to 0.625
- proj_bias: float32 [192], replicated, may hold values from -3 to 3
- dest_group: int32 [4, 32], replicated, may hold values from -1 to 3, as said below
- dest_slot: int32 [4, 32], replicated, may hold values from -1 to 3, as said below
Outputs:
- packed: bfloat16 [4, 8, 4, 192, 32, 128], P('clips', 'tm', None, None, 'tile')
The draws below stay inside these ranges and needn't reach their ends.
Inputs may be any that keep to these rules, and one draw needn't show every extreme that they name: `dest_group`: -1 marks the frames past their clip's end; each clip's live frames are its first ones, at least (100) // 5 of them, and one clip has all 32. A frame stays at its span index f // 4. From one span of one clip at most 2 frames go to any one group, and some span sends that many. `dest_slot`: -1 exactly where dest_group is -1. Frames that go to one group from one span index, over all clips, have distinct positions; some group receives 4 frames at some span index.
All inputs are finite; a program needn't handle non-finite values.
Results may differ from the reference program's by a relative error of at most 0.014.
Values may be sent and summed in bfloat16 or wider, within the bound.
A program may use at most 64 MiB of HBM per device.

```python
import math
import jax
import jax.numpy as jnp
from jax import lax

C = 96
C2 = 192
F_DEV = 4
COLS = 256
FRAMES = 32
ROWS = 64
CAP = 2
N_CLIPS = 4
N_TM = 8


def frame_plan(key):
    key_one, key_two, key_three = jax.random.split(key, 3)
    lowest = (3 * FRAMES + 4) // 5
    clip_lengths = jax.random.randint(key_one, (N_CLIPS,), lowest, FRAMES + 1)
    longest = jax.random.randint(key_two, (), 0, N_CLIPS)
    clip_lengths = jnp.where(jnp.arange(N_CLIPS) == longest, FRAMES, clip_lengths).astype(jnp.int32)
    rotation = jax.random.randint(key_three, (N_TM, 1), 0, N_CLIPS)
    frame_index = jnp.arange(N_TM)[:, None, None] * F_DEV + jnp.arange(F_DEV)[None, None, :]
    frame_live = frame_index < clip_lengths[None, :, None]
    flat_live = frame_live.reshape(N_TM, N_CLIPS * F_DEV).astype(jnp.int32)
    arrival = jnp.cumsum(flat_live, axis=1) - flat_live
    bundle = arrival // CAP
    target = (bundle + rotation) % N_CLIPS
    position = bundle // N_CLIPS * CAP + arrival % CAP
    target = jnp.where(flat_live > 0, target, -1)
    position = jnp.where(flat_live > 0, position, -1)
    target = target.reshape(N_TM, N_CLIPS, F_DEV).transpose(1, 0, 2).reshape(N_CLIPS, FRAMES)
    position = position.reshape(N_TM, N_CLIPS, F_DEV).transpose(1, 0, 2).reshape(N_CLIPS, FRAMES)
    return (target.astype(jnp.int32), position.astype(jnp.int32))


def draw_dest_group(key, part):
    target, position = frame_plan(key)
    return target


def draw_dest_slot(key, part):
    target, position = frame_plan(key)
    return position


def draw_video(key, part):
    key = jax.random.fold_in(key, 11)
    key_one, key_two, key_three = jax.random.split(key, 3)
    full_shape = (N_CLIPS, FRAMES, C, ROWS, COLS)
    rising_frames = jnp.exp(math.log(3.0) * jnp.arange(FRAMES, dtype=jnp.float32) / FRAMES)
    rising_rows = jnp.exp(math.log(3.0) * jnp.arange(ROWS, dtype=jnp.float32) / ROWS)
    rising = rising_frames[None, :, None, None, None] * rising_rows[None, None, None, :, None]
    channel = jnp.exp(jax.random.uniform(key_two, (N_CLIPS, 1, C, 1, 1), jnp.float32, math.log(0.3), math.log(3.0)))
    roughness = jnp.exp(jax.random.uniform(key_three, (N_CLIPS, FRAMES, 1, ROWS, 1), jnp.float32, math.log(0.7), math.log(1.4)))
    raw_noise = jax.random.normal(key_one, full_shape, jnp.float32)
    return (raw_noise * rising * channel * roughness).astype(jnp.bfloat16)


def bell_draw(own_key, extent, width, reach, held_as=jnp.bfloat16):
    array = width * jax.random.normal(own_key, extent, jnp.float32)
    return jnp.clip(array, min=-reach, max=reach).astype(held_as)


def setup_inputs(seed: int = 0) -> dict:
    key_list = jax.random.split(jax.random.key(seed), 14)
    return {
        "video": draw_video(jax.random.fold_in(key_list[13], 71), 0),
        "norm1_gain": jnp.clip(1.0 + 0.18 * jax.random.normal(key_list[1], (C,), jnp.float32), 0.1, 1.9),
        "conv1_weight": bell_draw(key_list[2], (3, 3, 3, C, C), (9 * C) ** -0.5, 0.21875),
        "conv1_bias": bell_draw(key_list[3], (C,), 0.5, 3.0, jnp.float32),
        "norm2_gain": jnp.clip(1.0 + 0.18 * jax.random.normal(key_list[4], (C,), jnp.float32), 0.1, 1.9),
        "conv2_weight": bell_draw(key_list[5], (3, 3, 3, C, C), (9 * C) ** -0.5, 0.21875),
        "conv2_bias": bell_draw(key_list[6], (C,), 0.5, 3.0, jnp.float32),
        "down_weight": bell_draw(key_list[7], (3, 3, C, C), (9 * C) ** -0.5, 0.21875),
        "down_bias": bell_draw(key_list[8], (C,), 0.5, 3.0, jnp.float32),
        "proj_weight": bell_draw(key_list[9], (C2, C), C ** -0.5, 0.625),
        "proj_bias": bell_draw(key_list[10], (C2,), 0.5, 3.0, jnp.float32),
        "dest_group": draw_dest_group(jax.random.fold_in(key_list[13], 71), 0),
        "dest_slot": draw_dest_slot(jax.random.fold_in(key_list[13], 71), 0),
    }


epsilon = 1e-06

def norm_silu(values, gain):
    widened = values.astype(jnp.float32)
    mean_square = lax.optimization_barrier(jnp.mean(widened * widened, axis=1, keepdims=True))
    normed = widened * lax.rsqrt(mean_square + epsilon) * gain[None, :, None, None]
    return jax.nn.silu(normed).astype(jnp.bfloat16)

def causal_conv(activation, weight, bias_row):
    padded = jnp.pad(activation.astype(jnp.float32), ((2, 0), (0, 0), (1, 1), (1, 1)))
    weight_wide = weight.astype(jnp.float32)
    summed = jnp.zeros((FRAMES, C, ROWS, COLS), jnp.float32)
    for i in range(3):
        for j in range(3):
            for l in range(3):
                window = padded[i:i + FRAMES, :, j:j + ROWS, l:l + COLS]
                summed = summed + jnp.einsum('oc,fcrw->forw', weight_wide[i, j, l], window)
    return summed + bias_row[None, :, None, None]

def shrink(block, down_weight, down_bias, proj_weight, proj_bias):
    extended = jnp.pad(block.astype(jnp.float32), ((0, 0), (0, 0), (0, 1), (0, 1)))
    weight_wide = down_weight.astype(jnp.float32)
    summed = jnp.zeros((FRAMES, C, ROWS // 2, COLS // 2), jnp.float32)
    for j in range(3):
        for l in range(3):
            window = extended[:, :, j:j + ROWS:2, l:l + COLS:2]
            summed = summed + jnp.einsum('oc,fcrw->forw', weight_wide[j, l], window)
    reduced = (summed + down_bias[None, :, None, None]).astype(jnp.bfloat16)
    latent = jnp.einsum('oc,fcrw->forw', proj_weight.astype(jnp.float32), reduced.astype(jnp.float32))
    return (latent + proj_bias[None, :, None, None]).astype(jnp.bfloat16)

def reference(video, norm1_gain, conv1_weight, conv1_bias, norm2_gain, conv2_weight, conv2_bias, down_weight, down_bias, proj_weight, proj_bias, dest_group, dest_slot):

    def encode_clip(clip_frames):
        first_act = norm_silu(clip_frames, norm1_gain)
        inner = causal_conv(first_act, conv1_weight, conv1_bias).astype(jnp.bfloat16)
        second_act = norm_silu(inner, norm2_gain)
        block = (causal_conv(second_act, conv2_weight, conv2_bias) + clip_frames.astype(jnp.float32)).astype(jnp.bfloat16)
        return shrink(block, down_weight, down_bias, proj_weight, proj_bias)
    latents = lax.map(encode_clip, video)
    frame_index = jnp.broadcast_to(jnp.arange(FRAMES, dtype=jnp.int32)[None, :], (N_CLIPS, FRAMES))
    span_index = (frame_index // F_DEV).astype(jnp.int32)
    target_group = jnp.where(dest_group >= 0, dest_group, N_CLIPS).astype(jnp.int32)
    target_slot = jnp.where(dest_slot >= 0, dest_slot, 0).astype(jnp.int32)
    packed = jnp.zeros((N_CLIPS, N_TM, F_DEV, C2, ROWS // 2, COLS // 2), jnp.bfloat16)
    return packed.at[target_group, span_index, target_slot].set(latents, mode='drop')
```

```python
import functools

import jax
import jax.numpy as jnp
from jax import lax
from jax.experimental import pallas as pl
from jax.experimental.pallas import tpu as pltpu
from jax.sharding import PartitionSpec as P

MESH = pl.DeviceIdType.MESH
EPS = 1e-06
C, C2, H, W, HALF = 96, 192, 4, 256, 128
BF, F32 = jnp.bfloat16, jnp.float32


def dot(a, b):
    return jnp.dot(a, b, preferred_element_type=F32)


def kernel(
    sizes,
    dgh, dsh, video, g1h, b1h, g2h, b2h, bdh, bph, w1h, w2h, dh, ph,
    out,
    vraw, vh, vht, vt, vn, a1, a2, s_out, s_in, bl, red, p_out, p_in, sel, got,
    w1raw, w2raw, draw, pw, w1f, w1m, w1e, w2f, w2m, w2l, w2e, w2p, dw,
    perm, rows, prow, cols, pcol, dg, ds, lsem, ssem, rsem,
):
    n_clips, n_tm, n_tile = sizes
    g = lax.axis_index("clips")
    t = lax.axis_index("tm")
    k = lax.axis_index("tile")
    up = {"tile": lax.rem(k + n_tile - 1, n_tile)}
    down = {"tile": lax.rem(k + 1, n_tile)}
    later = {"tm": lax.rem(t + 1, n_tm)}
    before = {"tm": lax.rem(t + n_tm - 1, n_tm)}
    others = [{"clips": lax.rem(g + 1 + j, n_clips)} for j in range(n_clips - 1)]
    first_span = t == 0
    top = k == 0
    bottom = k == n_tile - 1

    copies = {}

    def send(name, src, dst, device):
        i = len(copies)
        copy = pltpu.make_async_remote_copy(
            src_ref=src, dst_ref=dst, send_sem=ssem.at[i], recv_sem=rsem.at[i],
            device_id=device, device_id_type=MESH,
        )
        copy.start()
        copies[name] = copy

    def arrived(name):
        copies[name].wait_recv()

    locals_ = {}

    def fetch(name, src, dst):
        copy = pltpu.make_async_copy(src, dst, lsem.at[len(locals_)])
        copy.start()
        locals_[name] = copy

    barrier = pltpu.get_barrier_semaphore()
    peers = [up, down, later, before] + others
    for peer in peers:
        pl.semaphore_signal(barrier, inc=1, device_id=peer, device_id_type=MESH)
    for f in (2, 3, 1, 0):
        fetch(("v", f), video.at[f], vraw.at[f])
    for i, vector in enumerate((g1h, b1h, g2h, b2h, bdh)):
        fetch(("row", i), vector, rows.at[i])
    fetch("prow", bph, prow)
    fetch("w1", w1h, w1raw)
    fetch("w2", w2h, w2raw)
    fetch("d", dh, draw)
    fetch("p", ph, pw)
    fetch("dg", dgh, dg)
    fetch("ds", dsh, ds)

    src_col = lax.broadcasted_iota(jnp.int32, (W, W), 0)
    dst_col = lax.broadcasted_iota(jnp.int32, (W, W), 1)
    want = jnp.where(dst_col < HALF, 2 * dst_col, 2 * dst_col - (W - 1))
    perm[...] = (src_col == want).astype(F32).astype(BF)

    def column(row):
        n = row.shape[1]
        eye = lax.broadcasted_iota(jnp.int32, (n, n), 0) == lax.broadcasted_iota(jnp.int32, (n, n), 1)
        col = jnp.sum(jnp.where(eye, row, 0.0), axis=1, keepdims=True)
        return jnp.broadcast_to(col, (n, HALF))

    for i in range(5):
        locals_[("row", i)].wait()
        cols[i] = column(rows[i])
    locals_["prow"].wait()
    pcol[...] = column(prow[...])

    lane = lax.broadcasted_iota(jnp.int32, (C, HALF), 1)

    def halves(x):
        return x[:, :HALF], x[:, HALF:]

    def norm_silu(x, gain):
        ms = jnp.sum(x * x, axis=0, keepdims=True) * (1.0 / C)
        n = x * (lax.rsqrt(ms + EPS) * 0.5) * gain
        return n + n * jnp.tanh(n)

    def conv_row(a, frames, w, r):
        x = jnp.concatenate([a[f, pl.ds(r, 3)].reshape(3 * C, W) for f in frames], axis=0)
        y = dot(w[...], x)
        y0e, y0o = halves(y[:C])
        y1e, y1o = halves(y[C : 2 * C])
        y2e, y2o = halves(y[2 * C :])
        even = y1e + y2o + jnp.where(lane == 0, 0.0, pltpu.roll(y0o, 1, 1))
        odd = y1o + y0e + jnp.where(lane == HALF - 1, 0.0, pltpu.roll(y2e, HALF - 1, 1))
        return even, odd

    def turn(raw, dst):
        v = jnp.swapaxes(raw, 0, 1).reshape(H * C, W)
        dst[...] = dot(v, perm[...]).astype(BF).reshape(H, C, W)

    def first_act(src, index, keep=None):
        gain = cols[0]
        for r in range(H):
            for side in range(2):
                s = pl.ds(HALF * side, HALF)
                x = norm_silu(src[r, :, s].astype(F32), gain)
                if keep is not None:
                    x = jnp.where(keep, x, 0.0)
                a1[index, r + 1, :, s] = x.astype(BF)

    def send_a1(i):
        send(("a1up", i), a1.at[i, 1], a1.at[i, 5], up)
        send(("a1down", i), a1.at[i, 4], a1.at[i, 0], down)

    def take_a1(i):
        arrived(("a1up", i))
        arrived(("a1down", i))

        @pl.when(top)
        def _():
            a1[i, 0] = jnp.zeros((C, W), BF)

        @pl.when(bottom)
        def _():
            a1[i, 5] = jnp.zeros((C, W), BF)

    def send_a2(f):
        send(("a2up", f), a2.at[f, pl.ds(1, 2)], a2.at[f, pl.ds(5, 2)], up)
        send(("a2down", f), a2.at[f, 4], a2.at[f, 0], down)

    def take_a2(f):
        arrived(("a2up", f))
        arrived(("a2down", f))

        @pl.when(top)
        def _():
            a2[f, 0] = jnp.zeros((C, W), BF)

        @pl.when(bottom)
        def _():
            a2[f, pl.ds(5, 2)] = jnp.zeros((2, C, W), BF)

    def second_act(f, r, even, odd):
        for side, x in enumerate((even, odd)):
            x = (x + cols[1]).astype(BF).astype(F32)
            a2[f, r + 1, :, pl.ds(HALF * side, HALF)] = norm_silu(x, cols[2]).astype(BF)

    pl.semaphore_wait(barrier, len(peers))
    send("v", video.at[3], vh, later)

    for f in (2, 3, 1, 0):
        locals_[("v", f)].wait()
        turn(vraw[f], vt.at[f])
        first_act(vt.at[f], f + 1)
        send_a1(f + 1)
        send(("vt", f), vt.at[f, 0], vn.at[f], up)

    def gather_taps(raw, taps):
        return jnp.concatenate([raw[3 * i + j] for i in taps for j in range(3)], axis=1)

    locals_["w1"].wait()
    w1e[...] = gather_taps(w1raw, (0,))
    take_a1(3)
    for r in range(H):
        even, odd = conv_row(a1, (3,), w1e, r)
        s_out[r, :, pl.ds(0, HALF)] = even.astype(BF)
        s_out[r, :, pl.ds(HALF, HALF)] = odd.astype(BF)
    send("s", s_out, s_in, later)

    w1f[...] = gather_taps(w1raw, (0, 1, 2))
    w1m[...] = gather_taps(w1raw, (1, 2))
    take_a1(4)
    take_a1(2)
    for r in range(H):
        second_act(3, r, *conv_row(a1, (2, 3, 4), w1f, r))
    send_a2(3)
    take_a1(1)
    for r in range(H):
        second_act(2, r, *conv_row(a1, (1, 2, 3), w1f, r))
    send_a2(2)

    locals_["w2"].wait()
    w2f[...] = gather_taps(w2raw, (0, 1, 2))
    w2p[...] = gather_taps(w2raw, (0, 1))
    w2m[...] = gather_taps(w2raw, (1, 2))
    w2e[...] = gather_taps(w2raw, (0,))
    w2l[...] = gather_taps(w2raw, (2,))
    locals_["d"].wait()
    dw[...] = jnp.concatenate([draw[i] for i in range(9)], axis=1)

    def block_row(slot, r, even, odd):
        if r == H:
            even = jnp.where(bottom, 0.0, even)
            odd = jnp.where(bottom, 0.0, odd)
        even = even.astype(BF).astype(F32)
        bl[slot, r, 0] = even.astype(BF)
        bl[slot, r, 1] = odd.astype(BF)
        bl[slot, r, 2] = jnp.where(lane == HALF - 1, 0.0, pltpu.roll(even, HALF - 1, 1)).astype(BF)

    def shrink(slot):
        x = jnp.concatenate([bl[slot, pl.ds(2 * q, 3)].reshape(9 * C, HALF) for q in range(2)], axis=1)
        return dot(dw[...], x)

    take_a2(3)
    take_a2(2)
    for r in range(H + 1):
        block_row(0, r, *conv_row(a2, (2, 3), w2p, r))
        block_row(1, r, *conv_row(a2, (3,), w2e, r))
    for i in range(2):
        p_out[i] = shrink(i).astype(BF)
    send("p", p_out, p_in, later)

    arrived("v")
    turn(vh[...], vht)
    first_act(vht, 0, jnp.logical_not(first_span))
    send_a1(0)
    take_a1(0)
    for r in range(H):
        second_act(1, r, *conv_row(a1, (0, 1, 2), w1f, r))
    send_a2(1)
    arrived("s")
    for r in range(H):
        even, odd = conv_row(a1, (0, 1), w1m, r)
        se, so = halves(jnp.where(first_span, 0.0, s_in[r].astype(F32)))
        second_act(0, r, even + se, odd + so)
    send_a2(0)

    for f in range(H):
        arrived(("vt", f))

    def block_frame(f, frames, w):
        for r in range(H + 1):
            even, odd = conv_row(a2, frames, w, r)
            ve, vo = halves((vt[f, r] if r < H else vn[f]).astype(F32))
            block_row(f, r, even + cols[3] + ve, odd + cols[3] + vo)

    bias = jnp.concatenate([cols[4], cols[4]], axis=1)
    take_a2(1)
    block_frame(3, (1, 2, 3), w2f)
    red[3] = (shrink(3) + bias).astype(BF)
    take_a2(0)
    block_frame(2, (0, 1, 2), w2f)
    red[2] = (shrink(2) + bias).astype(BF)
    block_frame(1, (0, 1), w2m)
    block_frame(0, (0,), w2l)
    arrived("p")
    for f in range(2):
        part = jnp.where(first_span, 0.0, p_in[f].astype(F32))
        red[f] = (shrink(f) + bias + part).astype(BF)

    locals_["dg"].wait()
    locals_["ds"].wait()

    def target(group, f):
        return dg[group, t * H + f]

    def rank(group, f):
        return sum((jnp.int32(target(group, e) == target(group, f)) for e in range(f)), jnp.int32(0))

    for j in range(n_clips - 1):
        group = lax.rem(g + 1 + j, n_clips)
        for slot in range(2):
            frame = jnp.int32(0)
            for f in range(H):
                mine = jnp.logical_and(target(g, f) == group, rank(g, f) == slot)
                frame = jnp.where(mine, f, frame)
            sel[j, slot] = red[frame]
    for j in (1, 0, 2):
        send(("x", j), sel.at[j], got.at[pl.ds(2 * j, 2)], others[j])
    for f in range(H):
        got[6 + f] = red[f]

    place = [jnp.int32(-1)] * H
    for j in range(n_clips):
        group = g if j == n_clips - 1 else lax.rem(g + n_clips - 1 - j, n_clips)
        for f in range(H):
            slot = jnp.int32(f) if j == n_clips - 1 else rank(group, f)
            here = target(group, f) == g
            position = ds[group, t * H + f]
            for p in range(H):
                place[p] = jnp.where(jnp.logical_and(here, position == p), 2 * j + slot, place[p])
    locals_["p"].wait()
    for j in range(n_clips - 1):
        arrived(("x", j))
    for p in range(H):
        x = got[jnp.maximum(place[p], 0)]
        y = dot(pw[...], x) + jnp.concatenate([pcol[...], pcol[...]], axis=1)
        y = jnp.where(place[p] >= 0, y, 0.0)
        out[p] = y.reshape(C2, 2, HALF).astype(BF)
    for copy in copies.values():
        copy.wait_send()


N_COPIES, N_FETCHES = 28, 16


def local(
    video, norm1_gain, conv1_weight, conv1_bias, norm2_gain, conv2_weight, conv2_bias,
    down_weight, down_bias, proj_weight, proj_bias, dest_group, dest_slot, sizes,
):
    vm = pl.BlockSpec(memory_space=pltpu.VMEM)
    hbm = pl.BlockSpec(memory_space=pltpu.HBM)
    row = lambda v: v.reshape(1, C)
    taps = 9 * C
    packed = pl.pallas_call(
        functools.partial(kernel, sizes),
        out_shape=jax.ShapeDtypeStruct((H, C2, 2, HALF), BF),
        in_specs=[hbm] * 13,
        out_specs=vm,
        scratch_shapes=[
            pltpu.VMEM((H, C, H, W), BF),
            pltpu.VMEM((C, H, W), BF),
            pltpu.VMEM((H, C, W), BF),
            pltpu.VMEM((H, H, C, W), BF),
            pltpu.VMEM((H, C, W), BF),
            pltpu.VMEM((H + 1, H + 2, C, W), BF),
            pltpu.VMEM((H, H + 3, C, W), BF),
            pltpu.VMEM((H, C, W), BF),
            pltpu.VMEM((H, C, W), BF),
            pltpu.VMEM((H, H + 1, 3, C, HALF), BF),
            pltpu.VMEM((H, C, W), BF),
            pltpu.VMEM((2, C, W), BF),
            pltpu.VMEM((2, C, W), BF),
            pltpu.VMEM((3, 2, C, W), BF),
            pltpu.VMEM((10, C, W), BF),
            pltpu.VMEM((9, 3 * C, C), BF),
            pltpu.VMEM((9, 3 * C, C), BF),
            pltpu.VMEM((9, C, C), BF),
            pltpu.VMEM((C2, C), BF),
            pltpu.VMEM((3 * C, taps), BF),
            pltpu.VMEM((3 * C, 6 * C), BF),
            pltpu.VMEM((3 * C, 3 * C), BF),
            pltpu.VMEM((3 * C, taps), BF),
            pltpu.VMEM((3 * C, 6 * C), BF),
            pltpu.VMEM((3 * C, 3 * C), BF),
            pltpu.VMEM((3 * C, 3 * C), BF),
            pltpu.VMEM((3 * C, 6 * C), BF),
            pltpu.VMEM((C, taps), BF),
            pltpu.VMEM((W, W), BF),
            pltpu.VMEM((5, 1, C), F32),
            pltpu.VMEM((1, C2), F32),
            pltpu.VMEM((5, C, HALF), F32),
            pltpu.VMEM((C2, HALF), F32),
            pltpu.SMEM((4, 32), jnp.int32),
            pltpu.SMEM((4, 32), jnp.int32),
            pltpu.SemaphoreType.DMA((N_FETCHES,)),
            pltpu.SemaphoreType.DMA((N_COPIES,)),
            pltpu.SemaphoreType.DMA((N_COPIES,)),
        ],
        compiler_params=pltpu.CompilerParams(
            collective_id=0, has_side_effects=True, vmem_limit_bytes=63 << 20
        ),
        cost_estimate=pl.CostEstimate(flops=5 * 10**9, bytes_accessed=3 << 20, transcendentals=1 << 20),
        name="encode",
    )(
        dest_group, dest_slot, video[0], row(norm1_gain), row(conv1_bias), row(norm2_gain),
        row(conv2_bias), row(down_bias), proj_bias.reshape(1, C2),
        conv1_weight.reshape(9, 3 * C, C), conv2_weight.reshape(9, 3 * C, C),
        down_weight.reshape(9, C, C), proj_weight,
    )
    return packed[None, None]


def solution(mesh):
    sizes = (mesh.shape["clips"], mesh.shape["tm"], mesh.shape["tile"])
    return jax.shard_map(
        functools.partial(local, sizes=sizes),
        mesh=mesh,
        in_specs=(P("clips", "tm", None, "tile", None),) + (P(),) * 12,
        out_specs=P("clips", "tm", None, None, "tile", None),
        check_vma=False,
    )
```

```python
import functools

import jax
import jax.numpy as jnp
from jax import lax
from jax.experimental import pallas as pl
from jax.experimental.pallas import tpu as pltpu
from jax.sharding import PartitionSpec as P

MESH = pl.DeviceIdType.MESH
EPS = 1e-06
C, C2, H, W, HALF = 96, 192, 4, 256, 128
BF, F32 = jnp.bfloat16, jnp.float32


def dot(a, b):
    return jnp.dot(a, b, preferred_element_type=F32)


def kernel(
    sizes,
    dgh, dsh, video, g1h, b1h, g2h, b2h, bdh, bph, w1h, w2h, dh, ph,
    out,
    vraw, vh, vht, vt, vn, a1, a2, s_out, s_in, bl, red, p_out, p_in, sel, got,
    w1raw, w2raw, draw, pw, w1f, w1m, w1e, w2f, w2m, w2l, w2e, w2p, dw,
    perm, rows, prow, cols, pcol, dg, ds, lsem, ssem, rsem,
):
    n_clips, n_tm, n_tile = sizes
    g = lax.axis_index("clips")
    t = lax.axis_index("tm")
    k = lax.axis_index("tile")
    top, bottom = k == 0, k == n_tile - 1
    first, last = t == 0, t == n_tm - 1
    up = ("tile", jnp.maximum(k - 1, 0), k > 0, k < n_tile - 1)
    down = ("tile", jnp.minimum(k + 1, n_tile - 1), k < n_tile - 1, k > 0)
    later = ("tm", jnp.minimum(t + 1, n_tm - 1), t < n_tm - 1, t > 0)
    before = ("tm", jnp.maximum(t - 1, 0), t > 0, t < n_tm - 1)
    others = [("clips", lax.rem(g + 1 + j, n_clips), None, None) for j in range(n_clips - 1)]

    def under(condition, act):
        if condition is None:
            act()
        else:
            pl.when(condition)(act)

    copies = {}

    def send(name, src, dst, way):
        axis, coordinate, sends, receives = way
        i = len(copies)
        copy = pltpu.make_async_remote_copy(
            src_ref=src, dst_ref=dst, send_sem=ssem.at[i], recv_sem=rsem.at[i],
            device_id={axis: coordinate}, device_id_type=MESH,
        )
        under(sends, copy.start)
        copies[name] = (copy, sends, receives)

    def arrived(name):
        copy, _, receives = copies[name]
        under(receives, copy.wait_recv)

    fetches = {}

    def fetch(name, src, dst):
        copy = pltpu.make_async_copy(src, dst, lsem.at[len(fetches)])
        copy.start()
        fetches[name] = copy

    barrier = pltpu.get_barrier_semaphore()
    for axis, coordinate, sends, _ in [up, down, later, before] + others:
        under(sends, functools.partial(
            pl.semaphore_signal, barrier, inc=1, device_id={axis: coordinate}, device_id_type=MESH
        ))
    for f in (2, 3, 1, 0):
        fetch(("v", f), video.at[f], vraw.at[f])
    for i, vector in enumerate((g1h, b1h, g2h, b2h, bdh)):
        fetch(("row", i), vector, rows.at[i])
    fetch("prow", bph, prow)
    fetch("w1", w1h, w1raw)
    fetch("w2", w2h, w2raw)
    fetch("d", dh, draw)
    fetch("p", ph, pw)
    fetch("dg", dgh, dg)
    fetch("ds", dsh, ds)

    @pl.when(top)
    def _():
        for f in range(H + 1):
            a1[f, 0] = jnp.zeros((C, W), BF)
        for f in range(H):
            a2[f, 0] = jnp.zeros((C, W), BF)

    @pl.when(bottom)
    def _():
        for f in range(H + 1):
            a1[f, 5] = jnp.zeros((C, W), BF)
        for f in range(H):
            a2[f, pl.ds(5, 2)] = jnp.zeros((2, C, W), BF)
            vn[f] = jnp.zeros((C, W), BF)

    @pl.when(first)
    def _():
        vh[...] = jnp.zeros(vh.shape, BF)
        s_in[...] = jnp.zeros(s_in.shape, BF)
        p_in[...] = jnp.zeros(p_in.shape, BF)

    src_col = lax.broadcasted_iota(jnp.int32, (W, W), 0)
    dst_col = lax.broadcasted_iota(jnp.int32, (W, W), 1)
    want = jnp.where(dst_col < HALF, 2 * dst_col, 2 * dst_col - (W - 1))
    perm[...] = (src_col == want).astype(F32).astype(BF)

    pl.semaphore_wait(
        barrier,
        len(others) + jnp.int32(k > 0) + jnp.int32(k < n_tile - 1) + jnp.int32(t > 0) + jnp.int32(t < n_tm - 1),
    )
    send("v", video.at[3], vh, later)

    def column(row):
        n = row.shape[1]
        eye = lax.broadcasted_iota(jnp.int32, (n, n), 0) == lax.broadcasted_iota(jnp.int32, (n, n), 1)
        col = jnp.sum(jnp.where(eye, row, 0.0), axis=1, keepdims=True)
        return jnp.broadcast_to(col, (n, HALF))

    for i in range(5):
        fetches[("row", i)].wait()
    for i in range(5):
        cols[i] = column(rows[i])

    lane = lax.broadcasted_iota(jnp.int32, (C, HALF), 1)

    def halves(x):
        return x[:, :HALF], x[:, HALF:]

    def norm_silu(x, gain):
        ms = jnp.sum(x * x, axis=0, keepdims=True) * (1.0 / C)
        n = x * (lax.rsqrt(ms + EPS) * 0.5) * gain
        return n + n * jnp.tanh(n)

    def conv_row(a, frames, w, r):
        x = jnp.concatenate([a[f, pl.ds(r, 3)].reshape(3 * C, W) for f in frames], axis=0)
        y = dot(w[...], x)
        y0e, y0o = halves(y[:C])
        y1e, y1o = halves(y[C : 2 * C])
        y2e, y2o = halves(y[2 * C :])
        even = y1e + y2o + jnp.where(lane == 0, 0.0, pltpu.roll(y0o, 1, 1))
        odd = y1o + y0e + jnp.where(lane == HALF - 1, 0.0, pltpu.roll(y2e, HALF - 1, 1))
        return even, odd

    def turn(raw, dst):
        v = jnp.swapaxes(raw, 0, 1).reshape(H * C, W)
        dst[...] = dot(v, perm[...]).astype(BF).reshape(H, C, W)

    def first_act(src, index):
        for r in range(H):
            for side in range(2):
                s = pl.ds(HALF * side, HALF)
                a1[index, r + 1, :, s] = norm_silu(src[r, :, s].astype(F32), cols[0]).astype(BF)

    def send_a1(i):
        send(("a1up", i), a1.at[i, 1], a1.at[i, 5], up)
        send(("a1down", i), a1.at[i, 4], a1.at[i, 0], down)

    def take_a1(i):
        arrived(("a1up", i))
        arrived(("a1down", i))

    def send_a2(f):
        send(("a2up", f), a2.at[f, pl.ds(1, 2)], a2.at[f, pl.ds(5, 2)], up)
        send(("a2down", f), a2.at[f, 4], a2.at[f, 0], down)

    def second_act(f, r, even, odd):
        for side, x in enumerate((even, odd)):
            x = (x + cols[1]).astype(BF).astype(F32)
            a2[f, r + 1, :, pl.ds(HALF * side, HALF)] = norm_silu(x, cols[2]).astype(BF)

    for f in (2, 3, 1, 0):
        fetches[("v", f)].wait()
        turn(vraw[f], vt.at[f])
        first_act(vt.at[f], f + 1)
        send_a1(f + 1)
        send(("vt", f), vt.at[f, 0], vn.at[f], up)

    def gather_taps(raw, taps):
        return jnp.concatenate([raw[3 * i + j] for i in taps for j in range(3)], axis=1)

    fetches["w1"].wait()
    w1e[...] = gather_taps(w1raw, (0,))
    w1f[...] = gather_taps(w1raw, (0, 1, 2))
    w1m[...] = gather_taps(w1raw, (1, 2))

    take_a1(3)
    for r in range(H):
        even, odd = conv_row(a1, (3,), w1e, r)
        s_out[r, :, pl.ds(0, HALF)] = even.astype(BF)
        s_out[r, :, pl.ds(HALF, HALF)] = odd.astype(BF)
    send("s", s_out, s_in, later)

    take_a1(4)
    take_a1(2)
    for r in (0, 1, 3):
        second_act(3, r, *conv_row(a1, (2, 3, 4), w1f, r))
    send_a2(3)
    second_act(3, 2, *conv_row(a1, (2, 3, 4), w1f, 2))
    take_a1(1)
    for r in (0, 1, 3):
        second_act(2, r, *conv_row(a1, (1, 2, 3), w1f, r))
    send_a2(2)
    second_act(2, 2, *conv_row(a1, (1, 2, 3), w1f, 2))

    arrived("v")
    turn(vh[...], vht)
    first_act(vht, 0)
    send_a1(0)

    fetches["w2"].wait()
    w2f[...] = gather_taps(w2raw, (0, 1, 2))
    w2p[...] = gather_taps(w2raw, (0, 1))
    w2m[...] = gather_taps(w2raw, (1, 2))
    w2e[...] = gather_taps(w2raw, (0,))
    w2l[...] = gather_taps(w2raw, (2,))
    fetches["d"].wait()
    dw[...] = jnp.concatenate([draw[i] for i in range(9)], axis=1)
    for r in (1, 2):
        second_act(1, r, *conv_row(a1, (0, 1, 2), w1f, r))

    def block_row(slot, r, even, odd):
        if r == H:
            even = jnp.where(bottom, 0.0, even)
            odd = jnp.where(bottom, 0.0, odd)
        even = even.astype(BF).astype(F32)
        bl[slot, r, 0] = even.astype(BF)
        bl[slot, r, 1] = odd.astype(BF)
        bl[slot, r, 2] = jnp.where(lane == HALF - 1, 0.0, pltpu.roll(even, HALF - 1, 1)).astype(BF)

    def shrink(slots, q):
        x = jnp.concatenate([bl[i, pl.ds(2 * q, 3)].reshape(9 * C, HALF) for i in slots], axis=1)
        return halves(dot(dw[...], x))

    for f in (3, 2):
        arrived(("a2up", f))
        arrived(("a2down", f))
    for r in range(H + 1):
        block_row(4, r, *conv_row(a2, (2, 3), w2p, r))
        block_row(5, r, *conv_row(a2, (3,), w2e, r))
    for q in range(2):
        for i, part in enumerate(shrink((4, 5), q)):
            p_out[q, i] = part.astype(BF)
    send("p", p_out, p_in, later)

    take_a1(0)
    for r in (0, 3):
        second_act(1, r, *conv_row(a1, (0, 1, 2), w1f, r))
    send_a2(1)

    def first_frame(r):
        even, odd = conv_row(a1, (0, 1), w1m, r)
        se, so = halves(s_in[r].astype(F32))
        second_act(0, r, even + se, odd + so)

    arrived("s")
    for r in (0, 1, 3):
        first_frame(r)
    send_a2(0)
    first_frame(2)

    fetches["dg"].wait()
    fetches["ds"].wait()

    def target(group, f):
        return dg[group, t * H + f]

    def rank(group, f):
        return sum((jnp.int32(target(group, e) == target(group, f)) for e in range(f)), jnp.int32(0))

    picks = []
    own = [(target(g, f), rank(g, f)) for f in range(H)]
    for j in range(n_clips - 1):
        group = lax.rem(g + 1 + j, n_clips)
        for slot in range(2):
            frame = jnp.int32(0)
            for f, (to, order) in enumerate(own):
                frame = jnp.where(jnp.logical_and(to == group, order == slot), f, frame)
            picks.append(frame)
    place = [jnp.int32(-1)] * H
    for j in range(n_clips):
        mine = j == n_clips - 1
        group = g if mine else lax.rem(g + n_clips - 1 - j, n_clips)
        for f in range(H):
            slot = jnp.int32(f) if mine else rank(group, f)
            here = target(group, f) == g
            position = ds[group, t * H + f]
            for p in range(H):
                place[p] = jnp.where(jnp.logical_and(here, position == p), 2 * j + slot, place[p])

    for f in range(H):
        arrived(("vt", f))

    def block(f, r):
        frames, w = {3: ((1, 2, 3), w2f), 2: ((0, 1, 2), w2f), 1: ((0, 1), w2m), 0: ((0,), w2l)}[f]
        even, odd = conv_row(a2, frames, w, r)
        ve, vo = halves((vt[f, r] if r < H else vn[f]).astype(F32))
        block_row(f, r, even + cols[3] + ve, odd + cols[3] + vo)

    def ship(q):
        for pair in ((3, 2), (1, 0)):
            for f, part in zip(pair, shrink(pair, q)):
                if f < 2:
                    part = part + p_in[q, f].astype(F32)
                part = (part + cols[4]).astype(BF)
                red[q, f] = part
                got[q, 6 + f] = part
        for j in range(n_clips - 1):
            for slot in range(2):
                sel[q, j, slot] = red[q, picks[2 * j + slot]]
        for j in (1, 0, 2):
            send(("x", q, j), sel.at[q, j], got.at[q, pl.ds(2 * j, 2)], others[j])

    for r in (1, 2):
        for f in (3, 2, 1, 0):
            block(f, r)
    arrived(("a2down", 1))
    arrived(("a2down", 0))
    for f in (3, 2, 1, 0):
        block(f, 0)
    arrived("p")
    ship(0)
    arrived(("a2up", 1))
    arrived(("a2up", 0))
    for r in (3, 4):
        for f in (3, 2, 1, 0):
            block(f, r)
    ship(1)

    fetches["prow"].wait()
    pcol[...] = column(prow[...])
    fetches["p"].wait()
    for q in range(2):
        for j in range(n_clips - 1):
            arrived(("x", q, j))
    bias = jnp.concatenate([pcol[...], pcol[...]], axis=1)
    for p in range(H):
        i = jnp.maximum(place[p], 0)
        y = dot(pw[...], jnp.concatenate([got[0, i], got[1, i]], axis=1)) + bias
        y = jnp.where(place[p] >= 0, y, 0.0)
        out[p] = y.reshape(C2, 2, HALF).astype(BF)
    for copy, sends, _ in copies.values():
        under(sends, copy.wait_send)


N_COPIES, N_FETCHES = 31, 16


def local(
    video, norm1_gain, conv1_weight, conv1_bias, norm2_gain, conv2_weight, conv2_bias,
    down_weight, down_bias, proj_weight, proj_bias, dest_group, dest_slot, sizes,
):
    vm = pl.BlockSpec(memory_space=pltpu.VMEM)
    hbm = pl.BlockSpec(memory_space=pltpu.HBM)
    row = lambda v: v.reshape(1, C)
    taps = 9 * C
    packed = pl.pallas_call(
        functools.partial(kernel, sizes),
        out_shape=jax.ShapeDtypeStruct((H, C2, 2, HALF), BF),
        in_specs=[hbm] * 13,
        out_specs=vm,
        scratch_shapes=[
            pltpu.VMEM((H, C, H, W), BF),
            pltpu.VMEM((C, H, W), BF),
            pltpu.VMEM((H, C, W), BF),
            pltpu.VMEM((H, H, C, W), BF),
            pltpu.VMEM((H, C, W), BF),
            pltpu.VMEM((H + 1, H + 2, C, W), BF),
            pltpu.VMEM((H, H + 3, C, W), BF),
            pltpu.VMEM((H, C, W), BF),
            pltpu.VMEM((H, C, W), BF),
            pltpu.VMEM((H + 2, H + 1, 3, C, HALF), BF),
            pltpu.VMEM((2, H, C, HALF), BF),
            pltpu.VMEM((2, 2, C, HALF), BF),
            pltpu.VMEM((2, 2, C, HALF), BF),
            pltpu.VMEM((2, 3, 2, C, HALF), BF),
            pltpu.VMEM((2, 10, C, HALF), BF),
            pltpu.VMEM((9, 3 * C, C), BF),
            pltpu.VMEM((9, 3 * C, C), BF),
            pltpu.VMEM((9, C, C), BF),
            pltpu.VMEM((C2, C), BF),
            pltpu.VMEM((3 * C, taps), BF),
            pltpu.VMEM((3 * C, 6 * C), BF),
            pltpu.VMEM((3 * C, 3 * C), BF),
            pltpu.VMEM((3 * C, taps), BF),
            pltpu.VMEM((3 * C, 6 * C), BF),
            pltpu.VMEM((3 * C, 3 * C), BF),
            pltpu.VMEM((3 * C, 3 * C), BF),
            pltpu.VMEM((3 * C, 6 * C), BF),
            pltpu.VMEM((C, taps), BF),
            pltpu.VMEM((W, W), BF),
            pltpu.VMEM((5, 1, C), F32),
            pltpu.VMEM((1, C2), F32),
            pltpu.VMEM((5, C, HALF), F32),
            pltpu.VMEM((C2, HALF), F32),
            pltpu.SMEM((4, 32), jnp.int32),
            pltpu.SMEM((4, 32), jnp.int32),
            pltpu.SemaphoreType.DMA((N_FETCHES,)),
            pltpu.SemaphoreType.DMA((N_COPIES,)),
            pltpu.SemaphoreType.DMA((N_COPIES,)),
        ],
        compiler_params=pltpu.CompilerParams(
            collective_id=0, has_side_effects=True, vmem_limit_bytes=63 << 20
        ),
        cost_estimate=pl.CostEstimate(flops=5 * 10**9, bytes_accessed=3 << 20, transcendentals=1 << 20),
        name="encode",
    )(
        dest_group, dest_slot, video[0], row(norm1_gain), row(conv1_bias), row(norm2_gain),
        row(conv2_bias), row(down_bias), proj_bias.reshape(1, C2),
        conv1_weight.reshape(9, 3 * C, C), conv2_weight.reshape(9, 3 * C, C),
        down_weight.reshape(9, C, C), proj_weight,
    )
    return packed[None, None]


def solution(mesh):
    sizes = (mesh.shape["clips"], mesh.shape["tm"], mesh.shape["tile"])
    return jax.shard_map(
        functools.partial(local, sizes=sizes),
        mesh=mesh,
        in_specs=(P("clips", "tm", None, "tile", None),) + (P(),) * 12,
        out_specs=P("clips", "tm", None, None, "tile", None),
        check_vma=False,
    )
```

```python
import functools

import jax
import jax.numpy as jnp
from jax import lax
from jax.experimental import pallas as pl
from jax.experimental.pallas import tpu as pltpu
from jax.sharding import PartitionSpec as P

MESH = pl.DeviceIdType.MESH
EPS = 1e-06
C, C2, H, W, HALF = 96, 192, 4, 256, 128
BF, F32 = jnp.bfloat16, jnp.float32


def dot(a, b):
    return jnp.dot(a, b, preferred_element_type=F32)


def column(row):
    n = row.shape[1]
    eye = lax.broadcasted_iota(jnp.int32, (n, n), 0) == lax.broadcasted_iota(jnp.int32, (n, n), 1)
    col = jnp.sum(jnp.where(eye, row, 0.0), axis=1, keepdims=True)
    return jnp.broadcast_to(col, (n, HALF))


def kernel(
    sizes,
    dgh, dsh, video, g1h, b1h, g2h, b2h, bdh, w1h, w2h, dh,
    out,
    vraw, vh, vht, vt, vn, a1, a2, s_out, s_in, part, bl, red, p_out, p_in, sel, got,
    w1raw, w2raw, draw, w1f, w1m, w1e, w2f, w2m, w2l, w2e, w2p, dw,
    perm, rows, cols, dg, ds, lsem, ssem, rsem,
):
    n_clips, n_tm, n_tile = sizes
    g = lax.axis_index("clips")
    t = lax.axis_index("tm")
    k = lax.axis_index("tile")
    top, bottom = k == 0, k == n_tile - 1
    first, last = t == 0, t == n_tm - 1
    ways = {
        "up": ("tile", jnp.maximum(k - 1, 0), k > 0, k < n_tile - 1),
        "down": ("tile", jnp.minimum(k + 1, n_tile - 1), k < n_tile - 1, k > 0),
        "later": ("tm", jnp.minimum(t + 1, n_tm - 1), t < n_tm - 1, t > 0),
        "before": ("tm", jnp.maximum(t - 1, 0), t > 0, t < n_tm - 1),
    }
    for j in range(n_clips - 1):
        ways[j] = ("clips", lax.rem(g + 1 + j, n_clips), None, None)

    def under(condition, act):
        if condition is None:
            act()
        else:
            pl.when(condition)(act)

    copies = {}

    def send(way, **parts):
        axis, coordinate, sends, _ = ways[way]
        group = []
        for name, (src, dst) in parts.items():
            i = len(copies)
            copy = pltpu.make_async_remote_copy(
                src_ref=src, dst_ref=dst, send_sem=ssem.at[i], recv_sem=rsem.at[i],
                device_id={axis: coordinate}, device_id_type=MESH,
            )
            copies[name] = (copy, way)
            group.append(copy)

        def start():
            for copy in group:
                copy.start()

        under(sends, start)

    def each_way(names, side, act):
        for way in ways:
            group = [copies[name][0] for name in names if copies[name][1] == way]

            def run(group=group):
                for copy in group:
                    act(copy)

            if group:
                under(ways[way][side], run)

    def arrived(*names):
        each_way(names, 3, lambda copy: copy.wait_recv())

    fetches = {}

    def fetch(name, src, dst):
        copy = pltpu.make_async_copy(src, dst, lsem.at[len(fetches)])
        copy.start()
        fetches[name] = copy

    barrier = pltpu.get_barrier_semaphore()
    for axis, coordinate, sends, _ in ways.values():
        under(sends, functools.partial(
            pl.semaphore_signal, barrier, inc=1, device_id={axis: coordinate}, device_id_type=MESH
        ))
    for f in (2, 3, 1, 0):
        fetch(("v", f), video.at[f], vraw.at[f])
    for i, vector in enumerate((g1h, b1h, g2h, b2h, bdh)):
        fetch(("row", i), vector, rows.at[i])
    fetch("w1", w1h, w1raw)
    fetch("w2", w2h, w2raw)
    fetch("d", dh, draw)
    fetch("dg", dgh, dg)
    fetch("ds", dsh, ds)

    @pl.when(top)
    def _():
        for f in range(H + 1):
            a1[f, 0] = jnp.zeros((C, W), BF)
        for f in range(H):
            a2[f, 0] = jnp.zeros((C, W), BF)

    @pl.when(bottom)
    def _():
        for f in range(H + 1):
            a1[f, 5] = jnp.zeros((C, W), BF)
        for f in range(H):
            a2[f, pl.ds(5, 2)] = jnp.zeros((2, C, W), BF)
            vn[f] = jnp.zeros((C, W), BF)

    @pl.when(first)
    def _():
        vh[...] = jnp.zeros(vh.shape, BF)
        s_in[...] = jnp.zeros(s_in.shape, BF)
        p_in[...] = jnp.zeros(p_in.shape, BF)

    src_col = lax.broadcasted_iota(jnp.int32, (W, W), 0)
    dst_col = lax.broadcasted_iota(jnp.int32, (W, W), 1)
    want = jnp.where(dst_col < HALF, 2 * dst_col, 2 * dst_col - (W - 1))
    perm[...] = (src_col == want).astype(F32).astype(BF)

    pl.semaphore_wait(
        barrier,
        n_clips - 1 + jnp.int32(k > 0) + jnp.int32(k < n_tile - 1) + jnp.int32(t > 0) + jnp.int32(t < n_tm - 1),
    )
    send("later", v=(video.at[3], vh))

    for i in range(5):
        fetches[("row", i)].wait()
    for i in range(5):
        cols[i] = column(rows[i])

    lane = lax.broadcasted_iota(jnp.int32, (C, HALF), 1)

    def halves(x):
        return x[:, :HALF], x[:, HALF:]

    def norm_silu(x, gain):
        ms = jnp.sum(x * x, axis=0, keepdims=True) * (1.0 / C)
        n = x * (lax.rsqrt(ms + EPS) * 0.5) * gain
        return n + n * jnp.tanh(n)

    def conv_row(a, frames, w, r):
        x = jnp.concatenate([a[f, pl.ds(r, 3)].reshape(3 * C, W) for f in frames], axis=0)
        y = dot(w[...], x)
        y0e, y0o = halves(y[:C])
        y1e, y1o = halves(y[C : 2 * C])
        y2e, y2o = halves(y[2 * C :])
        even = y1e + y2o + jnp.where(lane == 0, 0.0, pltpu.roll(y0o, 1, 1))
        odd = y1o + y0e + jnp.where(lane == HALF - 1, 0.0, pltpu.roll(y2e, HALF - 1, 1))
        return even, odd

    def turn(raw, dst):
        v = jnp.swapaxes(raw, 0, 1).reshape(H * C, W)
        dst[...] = dot(v, perm[...]).astype(BF).reshape(H, C, W)

    def first_act(src, index):
        for r in range(H):
            for side in range(2):
                s = pl.ds(HALF * side, HALF)
                a1[index, r + 1, :, s] = norm_silu(src[r, :, s].astype(F32), cols[0]).astype(BF)

    def send_a1(first, count):
        i = pl.ds(first, count)
        send("down", **{f"a1down{first}": (a1.at[i, 4], a1.at[i, 0])})
        send("up", **{f"a1up{first}": (a1.at[i, 1], a1.at[i, 5])})

    def send_a2(first, count):
        f = pl.ds(first, count)
        send("down", **{f"a2down{first}": (a2.at[f, 4], a2.at[f, 0])})
        send("up", **{f"a2up{first}": (a2.at[f, pl.ds(1, 2)], a2.at[f, pl.ds(5, 2)])})

    def second_act(f, r, even, odd):
        for side, x in enumerate((even, odd)):
            x = (x + cols[1]).astype(BF).astype(F32)
            a2[f, r + 1, :, pl.ds(HALF * side, HALF)] = norm_silu(x, cols[2]).astype(BF)

    for pair in ((2, 3), (0, 1)):
        for f in pair:
            fetches[("v", f)].wait()
        for f in pair:
            turn(vraw[f], vt.at[f])
            first_act(vt.at[f], f + 1)
        send_a1(pair[0] + 1, 2)
    send("up", vt=(vt.at[:, 0], vn))

    def gather_taps(raw, taps):
        return jnp.concatenate([raw[3 * i + j] for i in taps for j in range(3)], axis=1)

    fetches["w1"].wait()
    w1e[...] = gather_taps(w1raw, (0,))
    w1f[...] = gather_taps(w1raw, (0, 1, 2))
    w1m[...] = gather_taps(w1raw, (1, 2))

    def early_tap(r):
        even, odd = conv_row(a1, (3,), w1e, r)
        i = (2, 0, 1, 3)[r]
        s_out[i, :, pl.ds(0, HALF)] = even.astype(BF)
        s_out[i, :, pl.ds(HALF, HALF)] = odd.astype(BF)

    for r in (1, 2):
        early_tap(r)
    for r in (1, 2):
        second_act(3, r, *conv_row(a1, (2, 3, 4), w1f, r))
        second_act(2, r, *conv_row(a1, (1, 2, 3), w1f, r))
    send("later", s0=(s_out.at[pl.ds(0, 2)], s_in.at[pl.ds(0, 2)]))
    fetches["w2"].wait()
    fetches["d"].wait()
    w2f[...] = gather_taps(w2raw, (0, 1, 2))
    w2p[...] = gather_taps(w2raw, (0, 1))
    w2m[...] = gather_taps(w2raw, (1, 2))
    w2e[...] = gather_taps(w2raw, (0,))
    w2l[...] = gather_taps(w2raw, (2,))
    dw[...] = jnp.concatenate([draw[i] for i in range(9)], axis=1)

    arrived("a1down3", "a1up3", "a1down1", "a1up1")
    for r in (0, 3):
        early_tap(r)
    for r in (0, 3):
        second_act(3, r, *conv_row(a1, (2, 3, 4), w1f, r))
        second_act(2, r, *conv_row(a1, (1, 2, 3), w1f, r))
    send("later", s1=(s_out.at[pl.ds(2, 2)], s_in.at[pl.ds(2, 2)]))
    send_a2(2, 2)

    arrived("v")
    turn(vh[...], vht)
    first_act(vht, 0)
    send_a1(0, 1)

    for r in (1, 2):
        second_act(1, r, *conv_row(a1, (0, 1, 2), w1f, r))
        part[r - 1, 0], part[r - 1, 1] = conv_row(a1, (0, 1), w1m, r)

    def block_row(slot, r, even, odd):
        if r == H:
            even = jnp.where(bottom, 0.0, even)
            odd = jnp.where(bottom, 0.0, odd)
        even = even.astype(BF).astype(F32)
        bl[slot, r, 0] = even.astype(BF)
        bl[slot, r, 1] = odd.astype(BF)
        bl[slot, r, 2] = jnp.where(lane == HALF - 1, 0.0, pltpu.roll(even, HALF - 1, 1)).astype(BF)

    def shrink(slots, q):
        x = jnp.concatenate([bl[i, pl.ds(2 * q, 3)].reshape(9 * C, HALF) for i in slots], axis=1)
        return halves(dot(dw[...], x))

    def span_row(r):
        block_row(4, r, *conv_row(a2, (2, 3), w2p, r))
        block_row(5, r, *conv_row(a2, (3,), w2e, r))

    def span_part(q):
        for i, x in enumerate(shrink((4, 5), q)):
            p_out[q, i] = x.astype(BF)
        send("later", **{f"p{q}": (p_out.at[q], p_in.at[q])})

    for r in (1, 2):
        span_row(r)

    arrived("a1down0", "a1up0", "s0", "s1")
    for r in (0, 3):
        second_act(1, r, *conv_row(a1, (0, 1, 2), w1f, r))
    send_a2(1, 1)
    for r in (0, 3, 1, 2):
        even, odd = conv_row(a1, (0, 1), w1m, r) if r in (0, 3) else (part[r - 1, 0], part[r - 1, 1])
        se, so = halves(s_in[(2, 0, 1, 3)[r]].astype(F32))
        second_act(0, r, even + se, odd + so)
    send_a2(0, 1)

    arrived("a2down2", "a2up2")
    span_row(0)
    span_part(0)
    for r in (3, 4):
        span_row(r)
    span_part(1)

    fetches["dg"].wait()
    fetches["ds"].wait()

    def target(group, f):
        return dg[group, t * H + f]

    def rank(group, f):
        return sum((jnp.int32(target(group, e) == target(group, f)) for e in range(f)), jnp.int32(0))

    picks = []
    own = [(target(g, f), rank(g, f)) for f in range(H)]
    for j in range(n_clips - 1):
        group = lax.rem(g + 1 + j, n_clips)
        for slot in range(2):
            frame = jnp.int32(0)
            for f, (to, order) in enumerate(own):
                frame = jnp.where(jnp.logical_and(to == group, order == slot), f, frame)
            picks.append(frame)
    place = [jnp.int32(-1)] * H
    for j in range(n_clips):
        mine = j == n_clips - 1
        group = g if mine else lax.rem(g + n_clips - 1 - j, n_clips)
        for f in range(H):
            slot = jnp.int32(f) if mine else rank(group, f)
            here = target(group, f) == g
            position = ds[group, t * H + f]
            for p in range(H):
                place[p] = jnp.where(jnp.logical_and(here, position == p), 2 * j + slot, place[p])

    def block(f, r):
        frames, w = {3: ((1, 2, 3), w2f), 2: ((0, 1, 2), w2f), 1: ((0, 1), w2m), 0: ((0,), w2l)}[f]
        even, odd = conv_row(a2, frames, w, r)
        ve, vo = halves((vt[f, r] if r < H else vn[f]).astype(F32))
        block_row(f, r, even + cols[3] + ve, odd + cols[3] + vo)

    def ship(q):
        for pair in ((3, 2), (1, 0)):
            for f, part in zip(pair, shrink(pair, q)):
                if f < 2:
                    part = part + p_in[q, f].astype(F32)
                part = (part + cols[4]).astype(BF)
                red[q, f] = part
                got[q, 6 + f] = part
        for j in range(n_clips - 1):
            for slot in range(2):
                sel[q, j, slot] = red[q, picks[2 * j + slot]]
        for j in (1, 0, 2):
            send(j, **{f"x{q}{j}": (sel.at[q, j], got.at[q, pl.ds(2 * j, 2)])})

    for r in (1, 2):
        for f in (3, 2, 1, 0):
            block(f, r)
    arrived("vt", "a2down1", "a2down0", "p0")
    for f in (3, 2, 1, 0):
        block(f, 0)
    ship(0)
    arrived("a2up1", "a2up0", "p1")
    for r in (3, 4):
        for f in (3, 2, 1, 0):
            block(f, r)
    ship(1)

    for q in range(2):
        for j in range(n_clips - 1):
            arrived(f"x{q}{j}")
    for p in range(H):
        for q in range(2):
            x = got[q, jnp.maximum(place[p], 0)]
            out[p, q] = jnp.where(place[p] >= 0, x, jnp.zeros_like(x))
    each_way(copies, 2, lambda copy: copy.wait_send())


def project(n_clips, dgh, dsh, xh, ph, bh, out, dg, ds, x, pw, row, y, sem, osem):
    g = lax.axis_index("clips")
    t = lax.axis_index("tm")
    fetches = [
        pltpu.make_async_copy(src, dst, sem.at[i])
        for i, (src, dst) in enumerate(((dgh, dg), (dsh, ds), (xh, x), (ph, pw), (bh, row)))
    ]
    for copy in fetches:
        copy.start()
    for copy in fetches:
        copy.wait()
    bias = column(row[...])
    bias = jnp.concatenate([bias, bias], axis=1)
    stores = []
    for p in range(H):
        filled = jnp.int32(0)
        for group in range(n_clips):
            for f in range(H):
                here = jnp.logical_and(dg[group, t * H + f] == g, ds[group, t * H + f] == p)
                filled = jnp.where(here, 1, filled)
        z = dot(pw[...], jnp.concatenate([x[p, 0], x[p, 1]], axis=1)) + bias
        z = jnp.where(filled > 0, z, 0.0)
        y[p] = z.reshape(C2, 2, HALF).astype(BF)
        copy = pltpu.make_async_copy(y.at[p], out.at[p], osem.at[p])
        copy.start()
        stores.append(copy)
    for copy in stores:
        copy.wait()


N_COPIES, N_FETCHES = 24, 14


def local(
    video, norm1_gain, conv1_weight, conv1_bias, norm2_gain, conv2_weight, conv2_bias,
    down_weight, down_bias, proj_weight, proj_bias, dest_group, dest_slot, sizes,
):
    vm = pl.BlockSpec(memory_space=pltpu.VMEM)
    hbm = pl.BlockSpec(memory_space=pltpu.HBM)
    row = lambda v: v.reshape(1, C)
    taps = 9 * C
    reduced = pl.pallas_call(
        functools.partial(kernel, sizes),
        out_shape=jax.ShapeDtypeStruct((H, 2, C, HALF), BF),
        in_specs=[hbm] * 11,
        out_specs=vm,
        scratch_shapes=[
            pltpu.VMEM((H, C, H, W), BF),
            pltpu.VMEM((C, H, W), BF),
            pltpu.VMEM((H, C, W), BF),
            pltpu.VMEM((H, H, C, W), BF),
            pltpu.VMEM((H, C, W), BF),
            pltpu.VMEM((H + 1, H + 2, C, W), BF),
            pltpu.VMEM((H, H + 3, C, W), BF),
            pltpu.VMEM((H, C, W), BF),
            pltpu.VMEM((H, C, W), BF),
            pltpu.VMEM((2, 2, C, HALF), F32),
            pltpu.VMEM((H + 2, H + 1, 3, C, HALF), BF),
            pltpu.VMEM((2, H, C, HALF), BF),
            pltpu.VMEM((2, 2, C, HALF), BF),
            pltpu.VMEM((2, 2, C, HALF), BF),
            pltpu.VMEM((2, 3, 2, C, HALF), BF),
            pltpu.VMEM((2, 10, C, HALF), BF),
            pltpu.VMEM((9, 3 * C, C), BF),
            pltpu.VMEM((9, 3 * C, C), BF),
            pltpu.VMEM((9, C, C), BF),
            pltpu.VMEM((3 * C, taps), BF),
            pltpu.VMEM((3 * C, 6 * C), BF),
            pltpu.VMEM((3 * C, 3 * C), BF),
            pltpu.VMEM((3 * C, taps), BF),
            pltpu.VMEM((3 * C, 6 * C), BF),
            pltpu.VMEM((3 * C, 3 * C), BF),
            pltpu.VMEM((3 * C, 3 * C), BF),
            pltpu.VMEM((3 * C, 6 * C), BF),
            pltpu.VMEM((C, taps), BF),
            pltpu.VMEM((W, W), BF),
            pltpu.VMEM((5, 1, C), F32),
            pltpu.VMEM((5, C, HALF), F32),
            pltpu.SMEM((4, 32), jnp.int32),
            pltpu.SMEM((4, 32), jnp.int32),
            pltpu.SemaphoreType.DMA((N_FETCHES,)),
            pltpu.SemaphoreType.DMA((N_COPIES,)),
            pltpu.SemaphoreType.DMA((N_COPIES,)),
        ],
        compiler_params=pltpu.CompilerParams(
            collective_id=0, has_side_effects=True, vmem_limit_bytes=63 << 20
        ),
        cost_estimate=pl.CostEstimate(flops=5 * 10**9, bytes_accessed=3 << 20, transcendentals=1 << 20),
        name="encode",
    )(
        dest_group, dest_slot, video[0], row(norm1_gain), row(conv1_bias), row(norm2_gain),
        row(conv2_bias), row(down_bias),
        conv1_weight.reshape(9, 3 * C, C), conv2_weight.reshape(9, 3 * C, C),
        down_weight.reshape(9, C, C),
    )
    packed = pl.pallas_call(
        functools.partial(project, sizes[0]),
        out_shape=jax.ShapeDtypeStruct((H, C2, 2, HALF), BF),
        in_specs=[hbm] * 5,
        out_specs=hbm,
        scratch_shapes=[
            pltpu.SMEM((4, 32), jnp.int32),
            pltpu.SMEM((4, 32), jnp.int32),
            pltpu.VMEM((H, 2, C, HALF), BF),
            pltpu.VMEM((C2, C), BF),
            pltpu.VMEM((1, C2), F32),
            pltpu.VMEM((H, C2, 2, HALF), BF),
            pltpu.SemaphoreType.DMA((5,)),
            pltpu.SemaphoreType.DMA((H,)),
        ],
        compiler_params=pltpu.CompilerParams(vmem_limit_bytes=63 << 20),
        cost_estimate=pl.CostEstimate(flops=4 * 10**7, bytes_accessed=1 << 20, transcendentals=0),
        name="project",
    )(dest_group, dest_slot, reduced, proj_weight, proj_bias.reshape(1, C2))
    return packed[None, None]


def solution(mesh):
    sizes = (mesh.shape["clips"], mesh.shape["tm"], mesh.shape["tile"])
    return jax.shard_map(
        functools.partial(local, sizes=sizes),
        mesh=mesh,
        in_specs=(P("clips", "tm", None, "tile", None),) + (P(),) * 12,
        out_specs=P("clips", "tm", None, None, "tile", None),
        check_vma=False,
    )
```

```python
import functools

import jax
import jax.numpy as jnp
from jax import lax
from jax.experimental import pallas as pl
from jax.experimental.pallas import tpu as pltpu
from jax.sharding import PartitionSpec as P

MESH = pl.DeviceIdType.MESH
EPS = 1e-06
C, C2, H, W, HALF = 96, 192, 4, 256, 128
BF, F32 = jnp.bfloat16, jnp.float32


def dot(a, b):
    return jnp.dot(a, b, preferred_element_type=F32)


def column(row):
    n = row.shape[1]
    eye = lax.broadcasted_iota(jnp.int32, (n, n), 0) == lax.broadcasted_iota(jnp.int32, (n, n), 1)
    col = jnp.sum(jnp.where(eye, row, 0.0), axis=1, keepdims=True)
    return jnp.broadcast_to(col, (n, HALF))


def kernel(
    sizes,
    dgh, video, g1h, b1h, g2h, b2h, bdh, w1h, w2h, dh,
    got,
    vraw, vh, vht, vt, vn, a1, a2, s_out, s_in, part, bl, red, p_out, p_in, sel,
    w1raw, w2raw, draw, w1f, w1m, w1e, w2f, w2m, w2l, w2e, w2p, dw,
    perm, rows, cols, dg, lsem, ssem, rsem,
):
    n_clips, n_tm, n_tile = sizes
    g = lax.axis_index("clips")
    t = lax.axis_index("tm")
    k = lax.axis_index("tile")
    top, bottom = k == 0, k == n_tile - 1
    first, last = t == 0, t == n_tm - 1
    ways = {
        "up": ("tile", jnp.maximum(k - 1, 0), k > 0, k < n_tile - 1),
        "down": ("tile", jnp.minimum(k + 1, n_tile - 1), k < n_tile - 1, k > 0),
        "later": ("tm", jnp.minimum(t + 1, n_tm - 1), t < n_tm - 1, t > 0),
        "before": ("tm", jnp.maximum(t - 1, 0), t > 0, t < n_tm - 1),
    }
    for j in range(n_clips - 1):
        ways[j] = ("clips", lax.rem(g + 1 + j, n_clips), None, None)

    def under(condition, act):
        if condition is None:
            act()
        else:
            pl.when(condition)(act)

    copies = {}

    def send(way, **parts):
        axis, coordinate, sends, _ = ways[way]
        group = []
        for name, (src, dst) in parts.items():
            i = len(copies)
            copy = pltpu.make_async_remote_copy(
                src_ref=src, dst_ref=dst, send_sem=ssem.at[i], recv_sem=rsem.at[i],
                device_id={axis: coordinate}, device_id_type=MESH,
            )
            copies[name] = (copy, way)
            group.append(copy)

        def start():
            for copy in group:
                copy.start()

        under(sends, start)

    def each_way(names, side, act):
        for way in ways:
            group = [copies[name][0] for name in names if copies[name][1] == way]

            def run(group=group):
                for copy in group:
                    act(copy)

            if group:
                under(ways[way][side], run)

    def arrived(*names):
        each_way(names, 3, lambda copy: copy.wait_recv())

    fetches = {}

    def fetch(name, src, dst):
        copy = pltpu.make_async_copy(src, dst, lsem.at[len(fetches)])
        copy.start()
        fetches[name] = copy

    barrier = pltpu.get_barrier_semaphore()
    for axis, coordinate, sends, _ in ways.values():
        under(sends, functools.partial(
            pl.semaphore_signal, barrier, inc=1, device_id={axis: coordinate}, device_id_type=MESH
        ))
    for f in (2, 3, 1, 0):
        fetch(("v", f), video.at[f], vraw.at[f])
    for i, vector in enumerate((g1h, b1h, g2h, b2h, bdh)):
        fetch(("row", i), vector, rows.at[i])
    fetch("w1", w1h, w1raw)
    fetch("w2", w2h, w2raw)
    fetch("d", dh, draw)
    fetch("dg", dgh, dg)

    @pl.when(top)
    def _():
        for f in range(H + 1):
            a1[f, 0] = jnp.zeros((C, W), BF)
        for f in range(H):
            a2[f, 0] = jnp.zeros((C, W), BF)

    @pl.when(bottom)
    def _():
        for f in range(H + 1):
            a1[f, 5] = jnp.zeros((C, W), BF)
        for f in range(H):
            a2[f, pl.ds(5, 2)] = jnp.zeros((2, C, W), BF)
            vn[f] = jnp.zeros((C, W), BF)

    @pl.when(first)
    def _():
        vh[...] = jnp.zeros(vh.shape, BF)
        s_in[...] = jnp.zeros(s_in.shape, BF)
        p_in[...] = jnp.zeros(p_in.shape, BF)

    src_col = lax.broadcasted_iota(jnp.int32, (W, W), 0)
    dst_col = lax.broadcasted_iota(jnp.int32, (W, W), 1)
    want = jnp.where(dst_col < HALF, 2 * dst_col, 2 * dst_col - (W - 1))
    perm[...] = (src_col == want).astype(F32).astype(BF)

    pl.semaphore_wait(
        barrier,
        n_clips - 1 + jnp.int32(k > 0) + jnp.int32(k < n_tile - 1) + jnp.int32(t > 0) + jnp.int32(t < n_tm - 1),
    )
    send("later", v=(video.at[3], vh))

    fetches[("row", 0)].wait()
    cols[0] = column(rows[0])

    lane = lax.broadcasted_iota(jnp.int32, (C, HALF), 1)

    def halves(x):
        return x[:, :HALF], x[:, HALF:]

    def norm_silu(x, gain):
        ms = jnp.sum(x * x, axis=0, keepdims=True) * (1.0 / C)
        n = x * (lax.rsqrt(ms + EPS) * 0.5) * gain
        return n + n * jnp.tanh(n)

    def conv_row(a, frames, w, r):
        x = jnp.concatenate([a[f, pl.ds(r, 3)].reshape(3 * C, W) for f in frames], axis=0)
        y = dot(w[...], x)
        y0e, y0o = halves(y[:C])
        y1e, y1o = halves(y[C : 2 * C])
        y2e, y2o = halves(y[2 * C :])
        even = y1e + y2o + jnp.where(lane == 0, 0.0, pltpu.roll(y0o, 1, 1))
        odd = y1o + y0e + jnp.where(lane == HALF - 1, 0.0, pltpu.roll(y2e, HALF - 1, 1))
        return even, odd

    def turn(raw, dst):
        v = jnp.swapaxes(raw, 0, 1).reshape(H * C, W)
        dst[...] = dot(v, perm[...]).astype(BF).reshape(H, C, W)

    def first_act(src, index):
        for r in range(H):
            for side in range(2):
                s = pl.ds(HALF * side, HALF)
                a1[index, r + 1, :, s] = norm_silu(src[r, :, s].astype(F32), cols[0]).astype(BF)

    def send_a1(first, count):
        i = pl.ds(first, count)
        send("down", **{f"a1down{first}": (a1.at[i, 4], a1.at[i, 0])})
        send("up", **{f"a1up{first}": (a1.at[i, 1], a1.at[i, 5])})

    def send_a2(first, count):
        f = pl.ds(first, count)
        send("down", **{f"a2down{first}": (a2.at[f, 4], a2.at[f, 0])})
        send("up", **{f"a2up{first}": (a2.at[f, pl.ds(1, 2)], a2.at[f, pl.ds(5, 2)])})

    def second_act(f, r, even, odd):
        for side, x in enumerate((even, odd)):
            x = (x + cols[1]).astype(BF).astype(F32)
            a2[f, r + 1, :, pl.ds(HALF * side, HALF)] = norm_silu(x, cols[2]).astype(BF)

    for pair in ((2, 3), (0, 1)):
        for f in pair:
            fetches[("v", f)].wait()
        for f in pair:
            turn(vraw[f], vt.at[f])
            first_act(vt.at[f], f + 1)
        send_a1(pair[0] + 1, 2)
    send("up", vt=(vt.at[:, 0], vn))

    def gather_taps(raw, taps):
        return jnp.concatenate([raw[3 * i + j] for i in taps for j in range(3)], axis=1)

    fetches["w1"].wait()
    fetches["w2"].wait()
    fetches["d"].wait()
    for i in range(1, 5):
        fetches[("row", i)].wait()
    for i in range(1, 5):
        cols[i] = column(rows[i])
    w1e[...] = gather_taps(w1raw, (0,))
    w1f[...] = gather_taps(w1raw, (0, 1, 2))
    w1m[...] = gather_taps(w1raw, (1, 2))

    def early_tap(r):
        even, odd = conv_row(a1, (3,), w1e, r)
        i = (2, 0, 1, 3)[r]
        s_out[i, :, pl.ds(0, HALF)] = even.astype(BF)
        s_out[i, :, pl.ds(HALF, HALF)] = odd.astype(BF)

    for r in (1, 2):
        early_tap(r)
    for r in (1, 2):
        second_act(3, r, *conv_row(a1, (2, 3, 4), w1f, r))
        second_act(2, r, *conv_row(a1, (1, 2, 3), w1f, r))
    w2f[...] = gather_taps(w2raw, (0, 1, 2))
    w2p[...] = gather_taps(w2raw, (0, 1))
    w2m[...] = gather_taps(w2raw, (1, 2))
    w2e[...] = gather_taps(w2raw, (0,))
    w2l[...] = gather_taps(w2raw, (2,))
    dw[...] = jnp.concatenate([draw[i] for i in range(9)], axis=1)
    send("later", s0=(s_out.at[pl.ds(0, 2)], s_in.at[pl.ds(0, 2)]))

    arrived("a1down3", "a1up3", "a1down1", "a1up1")
    for r in (0, 3):
        early_tap(r)
    send("later", s1=(s_out.at[pl.ds(2, 2)], s_in.at[pl.ds(2, 2)]))

    arrived("v")
    turn(vh[...], vht)
    first_act(vht, 0)
    send_a1(0, 1)

    for r in (0, 3):
        second_act(3, r, *conv_row(a1, (2, 3, 4), w1f, r))
        second_act(2, r, *conv_row(a1, (1, 2, 3), w1f, r))
    send_a2(2, 2)

    for r in (1, 2):
        second_act(1, r, *conv_row(a1, (0, 1, 2), w1f, r))
        part[r - 1, 0], part[r - 1, 1] = conv_row(a1, (0, 1), w1m, r)

    def block_row(slot, r, even, odd):
        if r == H:
            even = jnp.where(bottom, 0.0, even)
            odd = jnp.where(bottom, 0.0, odd)
        even = even.astype(BF).astype(F32)
        bl[slot, r, 0] = even.astype(BF)
        bl[slot, r, 1] = odd.astype(BF)
        bl[slot, r, 2] = jnp.where(lane == HALF - 1, 0.0, pltpu.roll(even, HALF - 1, 1)).astype(BF)

    def shrink(slots, q):
        x = jnp.concatenate([bl[i, pl.ds(2 * q, 3)].reshape(9 * C, HALF) for i in slots], axis=1)
        return halves(dot(dw[...], x))

    def span_row(r):
        block_row(4, r, *conv_row(a2, (2, 3), w2p, r))
        block_row(5, r, *conv_row(a2, (3,), w2e, r))

    def span_part(q):
        for i, x in enumerate(shrink((4, 5), q)):
            p_out[q, i] = x.astype(BF)
        send("later", **{f"p{q}": (p_out.at[q], p_in.at[q])})

    for r in (1, 2):
        span_row(r)

    arrived("a1down0", "a1up0", "s0", "s1")
    for r in (0, 3):
        second_act(1, r, *conv_row(a1, (0, 1, 2), w1f, r))
    send_a2(1, 1)
    for r in (0, 3, 1, 2):
        even, odd = conv_row(a1, (0, 1), w1m, r) if r in (0, 3) else (part[r - 1, 0], part[r - 1, 1])
        se, so = halves(s_in[(2, 0, 1, 3)[r]].astype(F32))
        second_act(0, r, even + se, odd + so)
    send_a2(0, 1)

    arrived("a2down2", "a2up2")
    span_row(0)
    span_part(0)
    for r in (3, 4):
        span_row(r)
    span_part(1)

    fetches["dg"].wait()

    def target(group, f):
        return dg[group, t * H + f]

    def rank(group, f):
        return sum((jnp.int32(target(group, e) == target(group, f)) for e in range(f)), jnp.int32(0))

    picks = []
    own = [(target(g, f), rank(g, f)) for f in range(H)]
    for j in range(n_clips - 1):
        group = lax.rem(g + 1 + j, n_clips)
        for slot in range(2):
            frame = jnp.int32(0)
            for f, (to, order) in enumerate(own):
                frame = jnp.where(jnp.logical_and(to == group, order == slot), f, frame)
            picks.append(frame)

    def block(f, r):
        frames, w = {3: ((1, 2, 3), w2f), 2: ((0, 1, 2), w2f), 1: ((0, 1), w2m), 0: ((0,), w2l)}[f]
        even, odd = conv_row(a2, frames, w, r)
        ve, vo = halves((vt[f, r] if r < H else vn[f]).astype(F32))
        block_row(f, r, even + cols[3] + ve, odd + cols[3] + vo)

    def ship(q):
        for pair in ((3, 2), (1, 0)):
            for f, part in zip(pair, shrink(pair, q)):
                if f < 2:
                    part = part + p_in[q, f].astype(F32)
                part = (part + cols[4]).astype(BF)
                red[q, f] = part
        fetch(("own", q), red.at[q], got.at[q, pl.ds(6, H)])
        for j in range(n_clips - 1):
            for slot in range(2):
                sel[q, j, slot] = red[q, picks[2 * j + slot]]
        for j in (1, 0, 2):
            send(j, **{f"x{q}{j}": (sel.at[q, j], got.at[q, pl.ds(2 * j, 2)])})

    for r in (1, 2):
        for f in (3, 2, 1, 0):
            block(f, r)
    arrived("vt", "a2down1", "a2down0")
    for f in (3, 2, 1, 0):
        block(f, 0)
    arrived("p0")
    ship(0)
    arrived("a2up1", "a2up0")
    for r in (3, 4):
        for f in (3, 2, 1, 0):
            block(f, r)
    arrived("p1")
    ship(1)

    for q in range(2):
        for j in range(n_clips - 1):
            arrived(f"x{q}{j}")
    for q in range(2):
        fetches[("own", q)].wait()
    each_way(copies, 2, lambda copy: copy.wait_send())


def project(n_clips, dgh, dsh, xh, ph, bh, out, dg, ds, x, pw, row, y, sem, osem):
    g = lax.axis_index("clips")
    t = lax.axis_index("tm")
    fetches = [
        pltpu.make_async_copy(src, dst, sem.at[i])
        for i, (src, dst) in enumerate(((dgh, dg), (dsh, ds), (xh, x), (ph, pw), (bh, row)))
    ]
    for copy in fetches:
        copy.start()
    fetches[4].wait()
    bias = column(row[...])
    bias = jnp.concatenate([bias, bias], axis=1)
    fetches[0].wait()
    fetches[1].wait()

    def target(group, f):
        return dg[group, t * H + f]

    place = [jnp.int32(-1)] * H
    for j in range(n_clips):
        mine = j == n_clips - 1
        group = g if mine else lax.rem(g + n_clips - 1 - j, n_clips)
        slot = jnp.int32(0)
        for f in range(H):
            here = target(group, f) == g
            position = ds[group, t * H + f]
            source = jnp.int32(6 + f) if mine else 2 * j + slot
            for p in range(H):
                place[p] = jnp.where(jnp.logical_and(here, position == p), source, place[p])
            slot = slot + jnp.int32(here)
    fetches[3].wait()
    fetches[2].wait()
    stores = []
    for p in range(H):
        i = jnp.maximum(place[p], 0)
        z = dot(pw[...], jnp.concatenate([x[0, i], x[1, i]], axis=1)) + bias
        z = jnp.where(place[p] >= 0, z, 0.0)
        y[p] = z.reshape(C2, 2, HALF).astype(BF)
        copy = pltpu.make_async_copy(y.at[p], out.at[p], osem.at[p])
        copy.start()
        stores.append(copy)
    for copy in stores:
        copy.wait()


N_COPIES, N_FETCHES = 24, 15


def local(
    video, norm1_gain, conv1_weight, conv1_bias, norm2_gain, conv2_weight, conv2_bias,
    down_weight, down_bias, proj_weight, proj_bias, dest_group, dest_slot, sizes,
):
    hbm = pl.BlockSpec(memory_space=pltpu.HBM)
    row = lambda v: v.reshape(1, C)
    taps = 9 * C
    reduced = pl.pallas_call(
        functools.partial(kernel, sizes),
        out_shape=jax.ShapeDtypeStruct((2, 10, C, HALF), BF),
        in_specs=[hbm] * 10,
        out_specs=hbm,
        scratch_shapes=[
            pltpu.VMEM((H, C, H, W), BF),
            pltpu.VMEM((C, H, W), BF),
            pltpu.VMEM((H, C, W), BF),
            pltpu.VMEM((H, H, C, W), BF),
            pltpu.VMEM((H, C, W), BF),
            pltpu.VMEM((H + 1, H + 2, C, W), BF),
            pltpu.VMEM((H, H + 3, C, W), BF),
            pltpu.VMEM((H, C, W), BF),
            pltpu.VMEM((H, C, W), BF),
            pltpu.VMEM((2, 2, C, HALF), F32),
            pltpu.VMEM((H + 2, H + 1, 3, C, HALF), BF),
            pltpu.VMEM((2, H, C, HALF), BF),
            pltpu.VMEM((2, 2, C, HALF), BF),
            pltpu.VMEM((2, 2, C, HALF), BF),
            pltpu.VMEM((2, 3, 2, C, HALF), BF),
            pltpu.VMEM((9, 3 * C, C), BF),
            pltpu.VMEM((9, 3 * C, C), BF),
            pltpu.VMEM((9, C, C), BF),
            pltpu.VMEM((3 * C, taps), BF),
            pltpu.VMEM((3 * C, 6 * C), BF),
            pltpu.VMEM((3 * C, 3 * C), BF),
            pltpu.VMEM((3 * C, taps), BF),
            pltpu.VMEM((3 * C, 6 * C), BF),
            pltpu.VMEM((3 * C, 3 * C), BF),
            pltpu.VMEM((3 * C, 3 * C), BF),
            pltpu.VMEM((3 * C, 6 * C), BF),
            pltpu.VMEM((C, taps), BF),
            pltpu.VMEM((W, W), BF),
            pltpu.VMEM((5, 1, C), F32),
            pltpu.VMEM((5, C, HALF), F32),
            pltpu.SMEM((4, 32), jnp.int32),
            pltpu.SemaphoreType.DMA((N_FETCHES,)),
            pltpu.SemaphoreType.DMA((N_COPIES,)),
            pltpu.SemaphoreType.DMA((N_COPIES,)),
        ],
        compiler_params=pltpu.CompilerParams(
            collective_id=0, has_side_effects=True, vmem_limit_bytes=63 << 20
        ),
        cost_estimate=pl.CostEstimate(flops=5 * 10**9, bytes_accessed=3 << 20, transcendentals=1 << 20),
        name="encode",
    )(
        dest_group, video[0], row(norm1_gain), row(conv1_bias), row(norm2_gain),
        row(conv2_bias), row(down_bias),
        conv1_weight.reshape(9, 3 * C, C), conv2_weight.reshape(9, 3 * C, C),
        down_weight.reshape(9, C, C),
    )
    packed = pl.pallas_call(
        functools.partial(project, sizes[0]),
        out_shape=jax.ShapeDtypeStruct((H, C2, 2, HALF), BF),
        in_specs=[hbm] * 5,
        out_specs=hbm,
        scratch_shapes=[
            pltpu.SMEM((4, 32), jnp.int32),
            pltpu.SMEM((4, 32), jnp.int32),
            pltpu.VMEM((2, 10, C, HALF), BF),
            pltpu.VMEM((C2, C), BF),
            pltpu.VMEM((1, C2), F32),
            pltpu.VMEM((H, C2, 2, HALF), BF),
            pltpu.SemaphoreType.DMA((5,)),
            pltpu.SemaphoreType.DMA((H,)),
        ],
        compiler_params=pltpu.CompilerParams(vmem_limit_bytes=63 << 20),
        cost_estimate=pl.CostEstimate(flops=4 * 10**7, bytes_accessed=1 << 20, transcendentals=0),
        name="project",
    )(dest_group, dest_slot, reduced, proj_weight, proj_bias.reshape(1, C2))
    return packed[None, None]


def solution(mesh):
    sizes = (mesh.shape["clips"], mesh.shape["tm"], mesh.shape["tile"])
    return jax.shard_map(
        functools.partial(local, sizes=sizes),
        mesh=mesh,
        in_specs=(P("clips", "tm", None, "tile", None),) + (P(),) * 12,
        out_specs=P("clips", "tm", None, None, "tile", None),
        check_vma=False,
    )
```
